32 devices in a mesh: tri: 8 (over z, y), vir: 4 (over x, core).
Axes of the slice: x: 2, y: 2, z: 4, core: 2. Of those that a mesh axis runs over, the one named last changes fastest.
Arguments:
- amps: bfloat16 [24, 768, 768], P('tri', 'vir'), may hold values from -0.21875 to 0.21875
- vvvo: bfloat16 [24, 768, 128], P('tri', 'vir'), may hold values from -6 to 6
- occ_gap: float32 [16], replicated, may hold values from 0.3 to 1
- vir_gap: float32 [768], P('vir'), may hold values from 0.5 to 2
- pair_gap: float32 [128], replicated, may hold values from 0.5 to 2
- block_sizes: int32 [8], replicated, may hold values from 1 to 3, 16 in all
- roots: int32 [8], replicated, may hold values from 0 to 7, each once
- triples: int32 [96, 2], P('tri'), may hold values from 0 to 7
Outputs:
- density: float32 [768, 128], P('vir')
- grad: float32 [24, 768, 128], P('tri', 'vir')
The draws below stay inside these ranges and needn't reach their ends.
Inputs may be any that keep to these rules, and one draw needn't show every extreme that they name: `block_sizes`: block sizes sum to 16; at least one block has exactly 3 orbitals. `roots`: each tri index stores exactly one block. `triples`: block numbers; a pair may repeat a block.
All inputs are finite; a program needn't handle non-finite values.
Results may differ from the reference program's by a relative error of at most 0.0003.
Values may be sent and summed in bfloat16 or wider, within the bound.
A program may use at most 128 MiB of HBM per device.

```python
import math
import jax
import jax.numpy as jnp
import numpy as np
from jax import lax

NV = 768
NB = 128
BMAX = 3
TPO = 12
NOCC = 16
N_TRI = 8


def with_ends(result, stream_key, low, largest):
    shape = result.shape
    place = [jax.random.randint(jax.random.fold_in(stream_key, axis), (), 0, shape[axis]) for axis in range(len(shape))]
    result = result.at[tuple(place)].set(low)
    longest = shape.index(max(shape))
    place[longest] = (place[longest] + 1) % shape[longest]
    return result.at[tuple(place)].set(largest)


def block_scale(stream_key, dims, cuts, low, top_value):
    level = 1.0
    for dim, blocks in cuts:
        steps = jax.random.uniform(jax.random.fold_in(jax.random.fold_in(stream_key, 6), dim), (blocks,), jnp.float32, low / len(cuts), top_value / len(cuts))
        level = level * jnp.repeat(jnp.exp(steps), dims[dim] // blocks).reshape((-1,) + (1,) * (len(dims) - 1 - dim))
    return level


def split_up(amount, total, limit, skew):
    loads = [(1 << 20) // math.isqrt(rank ** skew) + 1 for rank in range(2, amount + 1)]
    surplus, holding = total - limit - (amount - 1), [1] * (amount - 1)
    while surplus > 0:
        movable = [i for i in range(amount - 1) if holding[i] < limit]
        pool, budget = sum([loads[i] for i in movable]), surplus
        for i in movable:
            extra = min(limit - holding[i], max(1, budget * loads[i] // pool), surplus)
            holding[i] = holding[i] + extra
            surplus = surplus - extra
    return np.array([limit] + holding)


def uneven_parts(stream_key, count, total, limit, lean):
    if count == 2:
        one = jax.random.randint(stream_key, (), max(1, total - limit), min(limit, total - 1) + 1)
        return jnp.stack([one, total - one])
    sizes = jnp.asarray(split_up(count, total, limit, lean), jnp.int32)
    couples = (count - 1) // 2
    donor, taker = sizes[1:1 + 2 * couples:2], sizes[2:2 + 2 * couples:2]
    slack = jnp.minimum(donor - 1, limit - taker)
    passed = jax.random.randint(jax.random.fold_in(stream_key, 1), (couples,), 0, 1 << 20) % (slack + 1)
    sizes = sizes.at[1:1 + 2 * couples:2].set(donor - passed).at[2:2 + 2 * couples:2].set(taker + passed)
    return sizes[jax.random.permutation(jax.random.fold_in(stream_key, 2), count)]


def bell_draw(stream_key, dims, scale, most, pieces=(), kind=jnp.bfloat16):
    entries = scale * jax.random.normal(stream_key, dims, jnp.float32)
    if pieces:
        entries = entries * block_scale(stream_key, dims, pieces, -0.22, 0.18)
    return jnp.clip(entries, -most, most).astype(kind)


def setup_inputs(seed: int = 0) -> dict:
    streams_of = jax.random.split(jax.random.key(seed), 9)
    amps = bell_draw(streams_of[0], (N_TRI * BMAX, NV, NV), NV ** -0.5, 0.21875, ((0, 8), (1, 4)))
    vvvo = bell_draw(streams_of[1], (N_TRI * BMAX, NV, NB), 1.0, 6.0, ((0, 8), (1, 4)))
    occ_gap = jnp.clip(jax.random.uniform(streams_of[2], (NOCC,), jnp.float32, 0.3, 1.0), 0.3, 1.0)
    vir_gap = jnp.clip(0.5 + 1.5 * jax.random.uniform(streams_of[3], (NV,), jnp.float32) ** block_scale(streams_of[3], (NV,), ((0, 4),), -0.2, 0.2), 0.5, 2.0)
    pair_gap = jnp.clip(jax.random.uniform(streams_of[4], (NB,), jnp.float32, 0.5, 2.0), 0.5, 2.0)
    block_sizes = uneven_parts(streams_of[5], N_TRI, NOCC, BMAX, 2).astype(jnp.int32)
    roots = jax.random.permutation(streams_of[6], N_TRI).astype(jnp.int32)
    triples = with_ends(jax.random.randint(streams_of[7], (N_TRI * TPO, 2), 0, N_TRI), jax.random.fold_in(streams_of[7], 1), 0, N_TRI - 1).astype(jnp.int32)
    return dict(amps=amps, vvvo=vvvo, occ_gap=occ_gap, vir_gap=vir_gap, pair_gap=pair_gap, block_sizes=block_sizes, roots=roots, triples=triples)


def reference(amps, vvvo, occ_gap, vir_gap, pair_gap, block_sizes, roots, triples):
    slot_ids = jnp.arange(BMAX, dtype=jnp.int32)
    offsets = (jnp.cumsum(block_sizes) - block_sizes).astype(jnp.int32)
    owned = jnp.argsort(roots).astype(jnp.int32)

    def owner_step(density, owner_index):
        kblock = owned[owner_index]
        integral_values = lax.dynamic_slice_in_dim(vvvo, (owner_index * BMAX).astype(jnp.int32), BMAX, 0).astype(jnp.float32)
        own_gaps = occ_gap[jnp.minimum(offsets[kblock] + slot_ids, NOCC - 1)]
        own_live = slot_ids < block_sizes[kblock]
        base_den = vir_gap[:, None, None] + own_gaps[None, :, None] + pair_gap[None, None, :]
        pair_rows = lax.dynamic_slice_in_dim(triples, (owner_index * TPO).astype(jnp.int32), TPO, 0)

        def one_pair(state, pair_row):
            density_acc, gradient_running_total = state
            integral_layers = []
            projected_block = []
            gap_values = []
            live_masks = []
            for which_side in range(2):
                block_id = pair_row[which_side]
                row_ids = roots[block_id] * BMAX + slot_ids
                amplitude_layer = jnp.take(amps, row_ids, axis=0).astype(jnp.float32)
                integral_layers.append(amplitude_layer)
                projected_block.append(jnp.einsum('flg,ugw->fluw', amplitude_layer, integral_values))
                gap_values.append(occ_gap[jnp.minimum(offsets[block_id] + slot_ids, NOCC - 1)])
                live_masks.append(slot_ids < block_sizes[block_id])
            full_den = base_den[None, None] + gap_values[0][:, None, None, None, None] + gap_values[1][None, :, None, None, None]
            live_mask = live_masks[0][:, None, None, None, None] & live_masks[1][None, :, None, None, None] & own_live[None, None, None, :, None]
            weighted = jnp.where(live_mask, projected_block[0][:, None] * projected_block[1][None] / full_den, 0.0)
            density_acc = density_acc + jnp.sum(weighted * weighted, axis=(0, 1, 3))
            gradient_running_total = gradient_running_total + jnp.einsum('rnw,rqnhe->hwe', integral_layers[0], weighted, precision=lax.Precision.HIGHEST)
            return (density_acc, gradient_running_total), None

        start_grad = jnp.zeros((BMAX, NV, NB), jnp.float32)
        (density, grad_rows), _ = lax.scan(one_pair, (density, start_grad), pair_rows)
        return density, grad_rows

    start_density = jnp.zeros((NV, NB), jnp.float32)
    density, grad_all = lax.scan(owner_step, start_density, jnp.arange(N_TRI, dtype=jnp.int32))
    density = density / float(N_TRI * TPO)
    return density, grad_all.reshape(N_TRI * BMAX, NV, NB)
```

```python
import functools

import jax
import jax.numpy as jnp
from jax import lax
from jax.experimental import pallas as pl
from jax.experimental.pallas import tpu as pltpu
from jax.sharding import PartitionSpec as P

BMAX = 3
MESH = pl.DeviceIdType.MESH


def gather_kernel(tri, vir, amps, vvvo, amps_all, vvvo_all, send_sem, recv_sem, vsend_sem, vrecv_sem, own_sem):
    t = lax.axis_index("tri")
    v = lax.axis_index("vir")
    depth = vvvo.shape[1]
    columns = amps.shape[2] // 2
    odd = t % 2
    place = odd * (tri - 1 - t // 2) + (1 - odd) * (t // 2)

    def owner_at(where):
        where = where % tri
        back = where // (tri // 2)
        return (1 - back) * 2 * where + back * (2 * (tri - 1 - where) + 1)

    toward = (owner_at(place + 1), owner_at(place + tri - 1))

    barrier = pltpu.get_barrier_semaphore()
    for other in toward:
        pl.semaphore_signal(barrier, inc=1, device_id=(other, v), device_id_type=MESH)
    for hop in range(1, vir):
        pl.semaphore_signal(barrier, inc=1, device_id=(t, (v + hop) % vir), device_id_type=MESH)
    pl.semaphore_wait(barrier, 2 + vir - 1)

    def ring_copy(way, step, slot, first):
        source = owner_at(place + tri - step) if way == 0 else owner_at(place + step)
        cols = pl.ds(way * columns, columns)
        landing = amps_all.at[source * BMAX + slot, :, cols]
        return pltpu.make_async_remote_copy(
            src_ref=amps.at[slot, :, cols] if first else landing,
            dst_ref=landing,
            send_sem=send_sem.at[way, step, slot],
            recv_sem=recv_sem.at[way, step, slot],
            device_id=(toward[way], v),
            device_id_type=MESH,
        )

    def arrival(way, step, slot):
        source = owner_at(place + tri - step - 1) if way == 0 else owner_at(place + step + 1)
        landing = amps_all.at[source * BMAX + slot, :, pl.ds(way * columns, columns)]
        return pltpu.make_async_remote_copy(
            src_ref=landing,
            dst_ref=landing,
            send_sem=send_sem.at[way, step, slot],
            recv_sem=recv_sem.at[way, step, slot],
            device_id=(toward[way], v),
            device_id_type=MESH,
        )

    pieces = [(slot, way) for slot in range(BMAX) for way in range(2)]
    for slot, way in pieces:
        ring_copy(way, 0, slot, True).start()

    def integral_copy(hop, holder, target):
        return pltpu.make_async_remote_copy(
            src_ref=vvvo,
            dst_ref=vvvo_all.at[:, pl.ds(holder * depth, depth), :],
            send_sem=vsend_sem.at[hop - 1],
            recv_sem=vrecv_sem.at[hop - 1],
            device_id=(t, target),
            device_id_type=MESH,
        )

    for hop in range(1, vir):
        integral_copy(hop, v, (v + hop) % vir).start()
    own_amps = pltpu.make_async_copy(amps, amps_all.at[pl.ds(t * BMAX, BMAX)], own_sem.at[0])
    own_vvvo = pltpu.make_async_copy(vvvo, vvvo_all.at[:, pl.ds(v * depth, depth), :], own_sem.at[1])
    own_amps.start()
    own_vvvo.start()

    def forward(step, carry):
        for slot, way in pieces:
            arrival(way, step - 1, slot).wait_recv()
            ring_copy(way, step, slot, False).start()
        return carry

    lax.fori_loop(1, tri - 1, forward, 0)
    for slot, way in pieces:
        arrival(way, tri - 2, slot).wait_recv()
    for slot, way in pieces:
        ring_copy(way, 0, slot, True).wait_send()

    def drain(step, carry):
        for slot, way in pieces:
            ring_copy(way, step, slot, False).wait_send()
        return carry

    lax.fori_loop(1, tri - 1, drain, 0)
    for hop in range(1, vir):
        integral_copy(hop, (v + vir - hop) % vir, (v + hop) % vir).wait_recv()
        integral_copy(hop, v, (v + hop) % vir).wait_send()
    own_amps.wait()
    own_vvvo.wait()


def contract_kernel(
    sizes, roots, triples, occ_gap, vir_gap, pair_gap, amps, vvvo,
    density, grad, offsets, used, proj, weights, base, total,
):
    tri = sizes.shape[0]
    pairs = triples.shape[0]
    occ_count = occ_gap.shape[0]
    rows = amps.shape[1]
    width = vvvo.shape[2]
    t = lax.axis_index("tri")

    def walk(b, carry):
        start, own = carry
        offsets[b] = start
        used[roots[b]] = 0
        return start + sizes[b], jnp.where(roots[b] == t, b, own)

    _, own = lax.fori_loop(0, tri, walk, (jnp.int32(0), jnp.int32(0)))
    own_size = sizes[own]

    def gap(b, slot):
        return occ_gap[jnp.minimum(offsets[b] + slot, occ_count - 1)]

    outer = vir_gap[...] + pair_gap[...]
    for k in range(BMAX):
        base[k] = outer + gap(own, k)

    table = jnp.concatenate([vvvo[k] for k in range(BMAX)], axis=1)

    def project(b, carry):
        def one(slot, inner):
            row = roots[b] * BMAX + slot
            product = jnp.dot(amps[row], table, preferred_element_type=jnp.float32)
            for k in range(BMAX):
                proj[row, k] = product[:, k * width:(k + 1) * width]
            return inner

        return lax.fori_loop(0, sizes[b], one, carry)

    lax.fori_loop(0, tri, project, 0)
    density[...] = jnp.zeros_like(density)
    total[...] = jnp.zeros_like(total)

    def mark(q, carry):
        left_root = roots[triples[q, 0]]

        @pl.when(used[left_root] == 0)
        def _():
            used[left_root] = 1
            for slot in range(BMAX):
                weights[left_root * BMAX + slot] = jnp.zeros(weights.shape[1:], jnp.float32)

        return carry

    lax.fori_loop(0, pairs, mark, 0)
    tile = 48
    scale = 1.0 / float(tri * pairs)

    def one_pair(q, carry):
        left, right = triples[q, 0], triples[q, 1]
        left_row, right_row = roots[left] * BMAX, roots[right] * BMAX
        for count in range(1, BMAX + 1):

            @pl.when(sizes[right] == count)
            def _():
                right_gaps = [gap(right, j) for j in range(count)]

                def one_k(k, inner):
                    def one_left(i, deepest):
                        row = left_row + i
                        left_gap = gap(left, i)
                        for first in range(0, rows, tile):
                            at = pl.ds(first, tile)
                            p = proj[row, k, at, :]
                            den = base[k, at, :]
                            squares = density[at, :]
                            summed = weights[row, k, at, :]
                            for j in range(count):
                                d = den + (left_gap + right_gaps[j])
                                r = pl.reciprocal(d, approx=True)
                                r = r * (2.0 - d * r)
                                y = p * proj[right_row + j, k, at, :] * r
                                squares = squares + y * y
                                summed = summed + y
                            density[at, :] = squares
                            weights[row, k, at, :] = summed
                        return deepest

                    return lax.fori_loop(0, sizes[left], one_left, inner)

                lax.fori_loop(0, own_size, one_k, 0)

        return carry

    lax.fori_loop(0, pairs, one_pair, 0)
    density[...] = density[...] * scale

    def contract(b, carry):
        @pl.when(used[b] == 1)
        def _():
            stacked = amps[pl.ds(b * BMAX, BMAX)].reshape(BMAX * rows, amps.shape[2])
            high, low = [], []
            for k in range(BMAX):
                w = weights[pl.ds(b * BMAX, BMAX), k].reshape(BMAX * rows, width)
                top = w.astype(jnp.bfloat16)
                high.append(top)
                low.append((w - top.astype(jnp.float32)).astype(jnp.bfloat16))
            total[...] += lax.dot_general(
                stacked,
                jnp.concatenate(high + low, axis=1),
                (((0,), (0,)), ((), ())),
                preferred_element_type=jnp.float32,
            )

        return carry

    lax.fori_loop(0, tri, contract, 0)
    for k in range(BMAX):
        upper = total[:, k * width:(k + 1) * width]
        lower = total[:, (BMAX + k) * width:(BMAX + k + 1) * width]
        grad[k] = upper + lower


def reduce_kernel(tri, vir, grad, dens, grad_out, dens_out, grad_in, dens_in, gsend, grecv, dsend, drecv):
    t = lax.axis_index("tri")
    v = lax.axis_index("vir")
    depth = grad_out.shape[1]
    steps = tri.bit_length() - 1

    def partner(step):
        far = 1 << step
        bit = (t // far) % 2
        return t + far * (1 - 2 * bit)

    barrier = pltpu.get_barrier_semaphore()
    for hop in range(1, vir):
        pl.semaphore_signal(barrier, inc=1, device_id=(t, (v + hop) % vir), device_id_type=MESH)
    for step in range(steps):
        pl.semaphore_signal(barrier, inc=1, device_id=(partner(step), v), device_id_type=MESH)
    pl.semaphore_wait(barrier, vir - 1 + steps)

    def slice_copy(hop):
        target = (v + hop) % vir
        return pltpu.make_async_remote_copy(
            src_ref=grad.at[:, pl.ds(pl.multiple_of(target * depth, 16), depth), :],
            dst_ref=grad_in.at[hop - 1],
            send_sem=gsend.at[hop - 1],
            recv_sem=grecv.at[hop - 1],
            device_id=(t, target),
            device_id_type=MESH,
        )

    def density_copy(step):
        return pltpu.make_async_remote_copy(
            src_ref=dens if step == 0 else dens_out.at[step - 1],
            dst_ref=dens_in.at[step],
            send_sem=dsend.at[step],
            recv_sem=drecv.at[step],
            device_id=(partner(step), v),
            device_id_type=MESH,
        )

    density_copy(0).start()
    for hop in range(1, vir):
        slice_copy(hop).start()
    held = dens[...]
    for step in range(steps):
        density_copy(step).wait_recv()
        held = held + dens_in[step]
        dens_out[step] = held
        if step + 1 < steps:
            density_copy(step + 1).start()
    grad_out[...] = grad[:, pl.ds(pl.multiple_of(v * depth, 16), depth), :]
    for hop in range(1, vir):
        slice_copy(hop).wait_recv()
        grad_out[...] += grad_in[hop - 1]
    for hop in range(1, vir):
        slice_copy(hop).wait_send()
    for step in range(steps):
        density_copy(step).wait_send()


def body(tri, vir, amps, vvvo, occ_gap, vir_gap, pair_gap, block_sizes, roots, triples):
    rows, full = amps.shape[1:]
    depth, width = vvvo.shape[1:]
    anywhere = pl.BlockSpec(memory_space=pl.ANY)
    in_vmem = pl.BlockSpec(memory_space=pltpu.VMEM)
    in_smem = pl.BlockSpec(memory_space=pltpu.SMEM)
    f32 = jnp.float32
    amps_all, vvvo_all = pl.pallas_call(
        functools.partial(gather_kernel, tri, vir),
        out_shape=(
            jax.ShapeDtypeStruct((tri * BMAX, rows, full), amps.dtype),
            jax.ShapeDtypeStruct((BMAX, full, width), vvvo.dtype),
        ),
        in_specs=[anywhere] * 2,
        out_specs=(anywhere, anywhere),
        scratch_shapes=[
            pltpu.SemaphoreType.DMA((2, tri - 1, BMAX)),
            pltpu.SemaphoreType.DMA((2, tri - 1, BMAX)),
            pltpu.SemaphoreType.DMA((vir - 1,)),
            pltpu.SemaphoreType.DMA((vir - 1,)),
            pltpu.SemaphoreType.DMA((2,)),
        ],
        compiler_params=pltpu.CompilerParams(collective_id=0, has_side_effects=True),
        name="gather_rows",
    )(amps, vvvo)
    density, grad = pl.pallas_call(
        contract_kernel,
        out_shape=(
            jax.ShapeDtypeStruct((rows, width), f32),
            jax.ShapeDtypeStruct((BMAX, full, width), f32),
        ),
        in_specs=[in_smem] * 4 + [in_vmem] * 4,
        out_specs=(in_vmem, in_vmem),
        scratch_shapes=[
            pltpu.SMEM((tri,), jnp.int32),
            pltpu.SMEM((tri,), jnp.int32),
            pltpu.VMEM((tri * BMAX, BMAX, rows, width), f32),
            pltpu.VMEM((tri * BMAX, BMAX, rows, width), f32),
            pltpu.VMEM((BMAX, rows, width), f32),
            pltpu.VMEM((full, 2 * BMAX * width), f32),
        ],
        compiler_params=pltpu.CompilerParams(vmem_limit_bytes=48 << 20),
        name="contract_pairs",
    )(block_sizes, roots, triples, occ_gap, vir_gap[:, None], pair_gap[None, :], amps_all, vvvo_all)
    steps = tri.bit_length() - 1
    grad_share, density_steps = pl.pallas_call(
        functools.partial(reduce_kernel, tri, vir),
        out_shape=(
            jax.ShapeDtypeStruct((BMAX, depth, width), f32),
            jax.ShapeDtypeStruct((steps, rows, width), f32),
        ),
        in_specs=[in_vmem] * 2,
        out_specs=(in_vmem, in_vmem),
        scratch_shapes=[
            pltpu.VMEM((vir - 1, BMAX, depth, width), f32),
            pltpu.VMEM((steps, rows, width), f32),
            pltpu.SemaphoreType.DMA((vir - 1,)),
            pltpu.SemaphoreType.DMA((vir - 1,)),
            pltpu.SemaphoreType.DMA((steps,)),
            pltpu.SemaphoreType.DMA((steps,)),
        ],
        compiler_params=pltpu.CompilerParams(
            collective_id=1, has_side_effects=True, vmem_limit_bytes=16 << 20
        ),
        name="reduce_sums",
    )(grad, density)
    return density_steps[steps - 1], grad_share


def solution(mesh):
    return jax.shard_map(
        functools.partial(body, mesh.shape["tri"], mesh.shape["vir"]),
        mesh=mesh,
        in_specs=(
            P("tri", "vir", None),
            P("tri", "vir", None),
            P(),
            P("vir"),
            P(),
            P(),
            P(),
            P("tri", None),
        ),
        out_specs=(P("vir", None), P("tri", "vir", None)),
        check_vma=False,
    )
```

```python
import functools

import jax
import jax.numpy as jnp
from jax import lax
from jax.experimental import pallas as pl
from jax.experimental.pallas import tpu as pltpu
from jax.sharding import PartitionSpec as P

BMAX = 3
MESH = pl.DeviceIdType.MESH


def bits_of(count):
    return count.bit_length() - 1


def gather_kernel(
    tri, vir, split, amps, vvvo, triples, amps_all, vvvo_all, triples_all,
    send_sem, recv_sem, psend_sem, precv_sem, vsend_sem, vrecv_sem, xsend_sem, xrecv_sem, own_sem,
):
    t = lax.axis_index("tri")
    v = lax.axis_index("vir")
    ring = tri // split
    part = t // ring
    member = t % ring
    other_owner = (t + ring) % tri
    depth = vvvo.shape[1]
    rows = amps.shape[1] // split
    columns = amps.shape[2] // 2
    odd = member % 2
    place = odd * (ring - 1 - member // 2) + (1 - odd) * (member // 2)

    def member_at(where):
        where = where % ring
        back = where // (ring // 2)
        return (1 - back) * 2 * where + back * (2 * (ring - 1 - where) + 1)

    toward = tuple(part * ring + member_at(place + step) for step in (1, ring - 1))

    barrier = pltpu.get_barrier_semaphore()
    for other in toward:
        pl.semaphore_signal(barrier, inc=1, device_id=(other, v), device_id_type=MESH)
    for hop in range(1, vir):
        pl.semaphore_signal(barrier, inc=1, device_id=(t, (v + hop) % vir), device_id_type=MESH)
    if split == 2:
        pl.semaphore_signal(barrier, inc=1, device_id=(other_owner, v), device_id_type=MESH)
    pl.semaphore_wait(barrier, 2 + vir - 1 + split - 1)

    def part_rows(which):
        return pl.ds(pl.multiple_of(which * rows, 16), rows)

    def ring_copy(e, way, step, slot, arriving=False, first=False):
        shift = step + 1 if arriving else step
        source = member_at(place + ring - shift) if way == 0 else member_at(place + shift)
        half = (part + e) % split
        cols = pl.ds(way * columns, columns)
        landing = amps_all.at[(half * ring + source) * BMAX + slot, :, cols]
        return pltpu.make_async_remote_copy(
            src_ref=amps.at[slot, part_rows(part), cols] if first else landing,
            dst_ref=landing,
            send_sem=send_sem.at[e, way, step, slot],
            recv_sem=recv_sem.at[e, way, step, slot],
            device_id=(toward[way], v),
            device_id_type=MESH,
        )

    def start_ring(e, step, slot):
        for way in range(2):
            ring_copy(e, way, step, slot, first=e == 0).start()

    def forward(e, step, slot):
        for way in range(2):
            ring_copy(e, way, step - 1, slot, arriving=True).wait_recv()
            ring_copy(e, way, step, slot).start()

    def partner_copy(slot, owner):
        return pltpu.make_async_remote_copy(
            src_ref=amps.at[slot, part_rows((part + 1) % split), :],
            dst_ref=amps_all.at[owner * BMAX + slot],
            send_sem=psend_sem.at[slot],
            recv_sem=precv_sem.at[slot],
            device_id=(other_owner, v),
            device_id_type=MESH,
        )

    def to_partner(index, source, landing):
        return pltpu.make_async_remote_copy(
            src_ref=source,
            dst_ref=landing,
            send_sem=xsend_sem.at[index],
            recv_sem=xrecv_sem.at[index],
            device_id=(other_owner, v),
            device_id_type=MESH,
        )

    def integral_place(e, holder):
        at = pl.ds(pl.multiple_of(holder * depth, 16), depth)
        return vvvo_all.at[pl.ds(e * BMAX, BMAX), at, :]

    def integral_copy(e, hop, holder):
        return pltpu.make_async_remote_copy(
            src_ref=vvvo if e == 0 else integral_place(e, v),
            dst_ref=integral_place(e, holder),
            send_sem=vsend_sem.at[e, hop - 1],
            recv_sem=vrecv_sem.at[e, hop - 1],
            device_id=(t, (v + hop) % vir),
            device_id_type=MESH,
        )

    across = []
    if split == 2:
        across = [
            to_partner(0, triples, triples_all.at[1]),
            to_partner(1, vvvo, integral_place(1, v)),
        ]
    for copy in across:
        copy.start()
    for slot in range(BMAX):
        start_ring(0, 0, slot)
        if split == 2:
            partner_copy(slot, t).start()
    for hop in range(1, vir):
        integral_copy(0, hop, v).start()
    own = [
        pltpu.make_async_copy(
            amps.at[:, part_rows(part), :], amps_all.at[pl.ds(t * BMAX, BMAX)], own_sem.at[0]
        ),
        pltpu.make_async_copy(vvvo, integral_place(0, v), own_sem.at[1]),
        pltpu.make_async_copy(triples, triples_all.at[0], own_sem.at[2]),
    ]
    for copy in own:
        copy.start()

    if split == 2:
        for copy in across:
            copy.wait_recv()
        for hop in range(1, vir):
            integral_copy(1, hop, v).start()
        order = [(44 * step + 15 * slot, 0, step, slot) for step in range(1, ring - 1) for slot in range(BMAX)]
        order += [(60 * (slot + 1) + 44 * step, 1, step, slot) for step in range(ring - 1) for slot in range(BMAX)]
        for _, e, step, slot in sorted(order):
            if step == 0:
                partner_copy(slot, other_owner).wait_recv()
                start_ring(1, 0, slot)
            else:
                forward(e, step, slot)
    else:
        def hop_on(step, carry):
            for slot in range(BMAX):
                forward(0, step, slot)
            return carry

        lax.fori_loop(1, ring - 1, hop_on, 0)

    for e in range(split):
        for slot in range(BMAX):
            for way in range(2):
                ring_copy(e, way, ring - 2, slot, arriving=True).wait_recv()
                ring_copy(e, way, 0, slot, first=e == 0).wait_send()

        def drain(step, carry):
            for slot in range(BMAX):
                for way in range(2):
                    ring_copy(e, way, step, slot).wait_send()
            return carry

        lax.fori_loop(1, ring - 1, drain, 0)
        for hop in range(1, vir):
            integral_copy(e, hop, (v + vir - hop) % vir).wait_recv()
            integral_copy(e, hop, v).wait_send()
    if split == 2:
        for copy in across:
            copy.wait_send()
        for slot in range(BMAX):
            partner_copy(slot, t).wait_send()
    for copy in own:
        copy.wait()


def contract_kernel(
    split, tri, sizes, roots, triples, occ_gap, vir_gap, pair_gap, amps, vvvo,
    density, grad, offsets, rows_in, proj, weights, base, row_sem,
):
    pairs = triples.shape[2] // 2
    occ_count = occ_gap.shape[0]
    rows = amps.shape[1]
    width = vvvo.shape[2]
    layers = split * BMAX
    t = lax.axis_index("tri")
    ring = tri // split

    def fetch(b, start):
        offsets[b] = start

        def one(slot, carry):
            pltpu.make_async_copy(
                amps.at[roots[b] * BMAX + slot], rows_in.at[start + slot], row_sem.at[start + slot]
            ).start()
            return carry

        lax.fori_loop(0, sizes[b], one, 0)
        return start + sizes[b]

    lax.fori_loop(0, tri, fetch, jnp.int32(0))

    def find(owner):
        return lax.fori_loop(
            0, tri, lambda b, found: jnp.where(roots[b] == owner, b, found), jnp.int32(0)
        )

    owned = [find((t + e * ring) % tri) for e in range(split)]
    outer = vir_gap[pl.ds(pl.multiple_of((t // ring) * rows, 8), rows), :] + pair_gap[...]
    for e in range(split):
        for k in range(BMAX):
            own_gap = occ_gap[jnp.minimum(offsets[owned[e]] + k, occ_count - 1)]
            base[e * BMAX + k] = outer + own_gap
    density[...] = jnp.zeros_like(density)
    weights[...] = jnp.zeros_like(weights)
    table = jnp.concatenate([vvvo[layer] for layer in range(layers)], axis=1)
    group = 768 // rows
    span = group * rows

    def stacked(g):
        return rows_in[pl.ds(g * group, group)].reshape(span, rows_in.shape[2])

    def project(g, carry):
        for r in range(group):
            o = g * group + r
            pltpu.make_async_copy(amps.at[0], rows_in.at[o], row_sem.at[o]).wait()
        proj[pl.ds(pl.multiple_of(g * span, span), span), :] = jnp.dot(
            stacked(g), table, preferred_element_type=jnp.float32
        )
        return carry

    lax.fori_loop(0, occ_count // group, project, 0)
    tile = 48
    scale = 1.0 / float(tri * pairs)

    def one_pair(e, q):
        left, right = triples[e, 0, 2 * q], triples[e, 0, 2 * q + 1]
        left_first, right_first = offsets[left], offsets[right]
        for count in range(1, BMAX + 1):

            @pl.when(sizes[right] == count)
            def _():
                right_gaps = [occ_gap[right_first + j] for j in range(count)]

                def one_k(k, carry):
                    layer = e * BMAX + k
                    lanes = pl.ds(pl.multiple_of(layer * width, width), width)

                    def one_left(i, inner):
                        o = left_first + i
                        left_gap = occ_gap[o]
                        for first in range(0, rows, tile):
                            at = pl.ds(first, tile)
                            here = pl.ds(pl.multiple_of(o * rows, 8) + first, tile)
                            p = proj[here, lanes]
                            den = base[layer, at, :]
                            squares = density[at, :]
                            summed = weights[here, lanes]
                            for j in range(count):
                                there = pl.ds(pl.multiple_of((right_first + j) * rows, 8) + first, tile)
                                d = den + (left_gap + right_gaps[j])
                                r = pl.reciprocal(d, approx=True)
                                r = r * (2.0 - d * r)
                                y = p * proj[there, lanes] * r
                                squares = squares + y * y
                                summed = summed + y
                            density[at, :] = squares
                            weights[here, lanes] = summed
                        return inner

                    return lax.fori_loop(0, sizes[left], one_left, carry)

                lax.fori_loop(0, sizes[owned[e]], one_k, 0)

    for e in range(split):

        def each(q, carry):
            one_pair(e, q)
            return carry

        lax.fori_loop(0, pairs, each, 0)
    density[...] = density[...] * scale

    def product(g):
        left = stacked(g)
        w = weights[pl.ds(g * span, span), :]
        top = w.astype(jnp.bfloat16)
        rest = (w - top.astype(jnp.float32)).astype(jnp.bfloat16)
        over_rows = (((0,), (0,)), ((), ()))
        return lax.dot_general(
            left, top, over_rows, preferred_element_type=jnp.float32
        ) + lax.dot_general(left, rest, over_rows, preferred_element_type=jnp.float32)

    grad[...] = product(0)
    for g in range(1, occ_count // group):
        grad[...] += product(g)


def reduce_kernel(tri, vir, split, grad, dens, grad_out, dens_out, *scratch):
    levels = bits_of(vir)
    came, sums = scratch[:levels], scratch[levels:2 * levels]
    from_partner, dens_in, dens_sum, gsend, grecv, psend, precv, dsend, drecv = scratch[2 * levels:]
    t = lax.axis_index("tri")
    v = lax.axis_index("vir")
    depth, width = grad_out.shape[1:]
    rows = dens.shape[0]
    ring = tri // split
    steps = bits_of(ring)
    other_owner = (t + ring) % tri
    part = t // ring

    def bit(number, level):
        return (number // (1 << level)) % 2

    def flipped(number, level):
        return number + (1 << level) * (1 - 2 * bit(number, level))

    barrier = pltpu.get_barrier_semaphore()
    for level in range(levels):
        pl.semaphore_signal(barrier, inc=1, device_id=(t, flipped(v, level)), device_id_type=MESH)
    for step in range(steps):
        pl.semaphore_signal(barrier, inc=1, device_id=(flipped(t, step), v), device_id_type=MESH)
    if split == 2:
        pl.semaphore_signal(barrier, inc=1, device_id=(other_owner, v), device_id_type=MESH)
    pl.semaphore_wait(barrier, levels + steps + split - 1)

    def lanes(chunk):
        return pl.ds(chunk * width, width)

    def slab(holder):
        return pl.ds(pl.multiple_of(holder * depth, 16), depth)

    def halving(level, chunk, j):
        away = 2 * j + 1 - bit(v, level)
        return pltpu.make_async_remote_copy(
            src_ref=grad.at[slab(away), lanes(chunk)] if level == 0 else sums[level - 1].at[chunk, away],
            dst_ref=came[level].at[chunk, j],
            send_sem=gsend.at[level, chunk, j],
            recv_sem=grecv.at[level, chunk, j],
            device_id=(t, flipped(v, level)),
            device_id_type=MESH,
        )

    def partner_copy(k):
        return pltpu.make_async_remote_copy(
            src_ref=sums[levels - 1].at[BMAX + k, 0],
            dst_ref=from_partner.at[k],
            send_sem=psend.at[k],
            recv_sem=precv.at[k],
            device_id=(other_owner, v),
            device_id_type=MESH,
        )

    def density_copy(step):
        return pltpu.make_async_remote_copy(
            src_ref=dens if step == 0 else dens_sum.at[step - 1],
            dst_ref=dens_in.at[step],
            send_sem=dsend.at[step],
            recv_sem=drecv.at[step],
            device_id=(flipped(t, step), v),
            device_id_type=MESH,
        )

    def part_copy(which):
        at = pl.ds(pl.multiple_of(which * rows, 8), rows)
        return pltpu.make_async_remote_copy(
            src_ref=dens_out.at[at, :],
            dst_ref=dens_out.at[at, :],
            send_sem=dsend.at[steps],
            recv_sem=drecv.at[steps],
            device_id=(other_owner, v),
            device_id_type=MESH,
        )

    chunks = [e * BMAX + k for e in reversed(range(split)) for k in range(BMAX)]
    for chunk in chunks:
        for j in range(vir // 2):
            halving(0, chunk, j).start()
    density_copy(0).start()
    for level in range(levels):
        if level:
            step = level - 1
            if step < steps:
                density_copy(step).wait_recv()
                dens_sum[step] = (dens[...] if step == 0 else dens_sum[step - 1]) + dens_in[step]
                if step + 1 < steps:
                    density_copy(step + 1).start()
        for chunk in chunks:
            for j in range(vir >> (level + 1)):
                halving(level, chunk, j).wait_recv()
                kept = 2 * j + bit(v, level)
                held = grad[slab(kept), lanes(chunk)] if level == 0 else sums[level - 1][chunk, kept]
                sums[level][chunk, j] = held + came[level][chunk, j]
            if level + 1 < levels:
                for j in range(vir >> (level + 2)):
                    halving(level + 1, chunk, j).start()
            elif chunk >= BMAX:
                partner_copy(chunk - BMAX).start()
    for step in range(max(levels - 1, 0), steps):
        density_copy(step).wait_recv()
        dens_sum[step] = (dens[...] if step == 0 else dens_sum[step - 1]) + dens_in[step]
        if step + 1 < steps:
            density_copy(step + 1).start()
    dens_out[pl.ds(pl.multiple_of(part * rows, 8), rows), :] = dens_sum[steps - 1]
    if split == 2:
        part_copy(part).start()
    for k in range(BMAX):
        if split == 2:
            partner_copy(k).wait_recv()
            grad_out[k] = sums[levels - 1][k, 0] + from_partner[k]
        else:
            grad_out[k] = sums[levels - 1][k, 0]
    for level in range(levels):
        for chunk in chunks:
            for j in range(vir >> (level + 1)):
                halving(level, chunk, j).wait_send()
    for step in range(steps):
        density_copy(step).wait_send()
    if split == 2:
        for k in range(BMAX):
            partner_copy(k).wait_send()
        part_copy(1 - part).wait_recv()
        part_copy(part).wait_send()


def body(tri, vir, amps, vvvo, occ_gap, vir_gap, pair_gap, block_sizes, roots, triples):
    own_rows, full = amps.shape[1:]
    depth, width = vvvo.shape[1:]
    pairs = triples.shape[0]
    occ_count = occ_gap.shape[0]
    split = 2 if own_rows % 32 == 0 and tri % 4 == 0 else 1
    ring = tri // split
    rows = own_rows // split
    layers = split * BMAX
    anywhere = pl.BlockSpec(memory_space=pl.ANY)
    in_vmem = pl.BlockSpec(memory_space=pltpu.VMEM)
    in_smem = pl.BlockSpec(memory_space=pltpu.SMEM)
    f32 = jnp.float32
    dma = pltpu.SemaphoreType.DMA
    amps_all, vvvo_all, triples_all = pl.pallas_call(
        functools.partial(gather_kernel, tri, vir, split),
        out_shape=(
            jax.ShapeDtypeStruct((tri * BMAX, rows, full), amps.dtype),
            jax.ShapeDtypeStruct((layers, full, width), vvvo.dtype),
            jax.ShapeDtypeStruct((split, 1, 2 * pairs), triples.dtype),
        ),
        in_specs=[anywhere] * 3,
        out_specs=(anywhere,) * 3,
        scratch_shapes=[
            dma((split, 2, ring - 1, BMAX)),
            dma((split, 2, ring - 1, BMAX)),
            dma((BMAX,)),
            dma((BMAX,)),
            dma((split, vir - 1)),
            dma((split, vir - 1)),
            dma((2,)),
            dma((2,)),
            dma((3,)),
        ],
        compiler_params=pltpu.CompilerParams(collective_id=0, has_side_effects=True),
        name="gather_rows",
    )(amps, vvvo, triples.reshape(1, 2 * pairs))
    density, grad = pl.pallas_call(
        functools.partial(contract_kernel, split, tri),
        out_shape=(
            jax.ShapeDtypeStruct((rows, width), f32),
            jax.ShapeDtypeStruct((full, layers * width), f32),
        ),
        in_specs=[in_smem] * 4 + [in_vmem] * 2 + [anywhere, in_vmem],
        out_specs=(in_vmem, in_vmem),
        scratch_shapes=[
            pltpu.SMEM((tri,), jnp.int32),
            pltpu.VMEM((occ_count, rows, full), amps.dtype),
            pltpu.VMEM((occ_count * rows, layers * width), f32),
            pltpu.VMEM((occ_count * rows, layers * width), f32),
            pltpu.VMEM((layers, rows, width), f32),
            dma((occ_count,)),
        ],
        compiler_params=pltpu.CompilerParams(vmem_limit_bytes=48 << 20),
        name="contract_pairs",
    )(block_sizes, roots, triples_all, occ_gap, vir_gap[:, None], pair_gap[None, :], amps_all, vvvo_all)
    steps = bits_of(ring)
    levels = bits_of(vir)
    halves = [(layers, vir >> (level + 1), depth, width) for level in range(levels)]
    grad_share, density_all = pl.pallas_call(
        functools.partial(reduce_kernel, tri, vir, split),
        out_shape=(
            jax.ShapeDtypeStruct((BMAX, depth, width), f32),
            jax.ShapeDtypeStruct((own_rows, width), f32),
        ),
        in_specs=[in_vmem] * 2,
        out_specs=(in_vmem, in_vmem),
        scratch_shapes=[pltpu.VMEM(shape, f32) for shape in halves + halves]
        + [
            pltpu.VMEM((BMAX, depth, width), f32),
            pltpu.VMEM((steps, rows, width), f32),
            pltpu.VMEM((steps, rows, width), f32),
            dma((levels, layers, vir // 2)),
            dma((levels, layers, vir // 2)),
            dma((BMAX,)),
            dma((BMAX,)),
            dma((steps + 1,)),
            dma((steps + 1,)),
        ],
        compiler_params=pltpu.CompilerParams(
            collective_id=1, has_side_effects=True, vmem_limit_bytes=24 << 20
        ),
        name="reduce_sums",
    )(grad, density)
    return density_all, grad_share


def solution(mesh):
    return jax.shard_map(
        functools.partial(body, mesh.shape["tri"], mesh.shape["vir"]),
        mesh=mesh,
        in_specs=(
            P("tri", "vir", None),
            P("tri", "vir", None),
            P(),
            P("vir"),
            P(),
            P(),
            P(),
            P("tri", None),
        ),
        out_specs=(P("vir", None), P("tri", "vir", None)),
        check_vma=False,
    )
```

```python
import functools

import jax
import jax.numpy as jnp
from jax import lax
from jax.experimental import pallas as pl
from jax.experimental.pallas import tpu as pltpu
from jax.sharding import PartitionSpec as P

BMAX = 3
MESH = pl.DeviceIdType.MESH


def bits_of(count):
    return count.bit_length() - 1


def gather_kernel(
    tri, vir, split, amps, vvvo, triples, amps_all, vvvo_all, triples_all,
    send_sem, recv_sem, psend_sem, precv_sem, vsend_sem, vrecv_sem, xsend_sem, xrecv_sem, own_sem,
):
    t = lax.axis_index("tri")
    v = lax.axis_index("vir")
    ring = tri // split
    part = t // ring
    member = t % ring
    other_owner = (t + ring) % tri
    depth = vvvo.shape[1]
    rows = amps.shape[1] // split
    columns = amps.shape[2] // 2
    odd = member % 2
    place = odd * (ring - 1 - member // 2) + (1 - odd) * (member // 2)

    def member_at(where):
        where = where % ring
        back = where // (ring // 2)
        return (1 - back) * 2 * where + back * (2 * (ring - 1 - where) + 1)

    toward = tuple(part * ring + member_at(place + step) for step in (1, ring - 1))

    barrier = pltpu.get_barrier_semaphore()
    for other in toward:
        pl.semaphore_signal(barrier, inc=1, device_id=(other, v), device_id_type=MESH)
    for hop in range(1, vir):
        pl.semaphore_signal(barrier, inc=1, device_id=(t, (v + hop) % vir), device_id_type=MESH)
    if split == 2:
        pl.semaphore_signal(barrier, inc=1, device_id=(other_owner, v), device_id_type=MESH)
    pl.semaphore_wait(barrier, 2 + vir - 1 + split - 1)

    def part_rows(which):
        return pl.ds(pl.multiple_of(which * rows, 16), rows)

    def ring_copy(e, way, step, slot, arriving=False, first=False):
        shift = step + 1 if arriving else step
        source = member_at(place + ring - shift) if way == 0 else member_at(place + shift)
        half = (part + e) % split
        cols = pl.ds(way * columns, columns)
        landing = amps_all.at[(half * ring + source) * BMAX + slot, :, cols]
        return pltpu.make_async_remote_copy(
            src_ref=amps.at[slot, part_rows(part), cols] if first else landing,
            dst_ref=landing,
            send_sem=send_sem.at[e, way, step, slot],
            recv_sem=recv_sem.at[e, way, step, slot],
            device_id=(toward[way], v),
            device_id_type=MESH,
        )

    def start_ring(e, step, slot):
        for way in range(2):
            ring_copy(e, way, step, slot, first=e == 0).start()

    def forward(e, step, slot):
        for way in range(2):
            ring_copy(e, way, step - 1, slot, arriving=True).wait_recv()
            ring_copy(e, way, step, slot).start()

    def partner_copy(slot, owner):
        return pltpu.make_async_remote_copy(
            src_ref=amps.at[slot, part_rows((part + 1) % split), :],
            dst_ref=amps_all.at[owner * BMAX + slot],
            send_sem=psend_sem.at[slot],
            recv_sem=precv_sem.at[slot],
            device_id=(other_owner, v),
            device_id_type=MESH,
        )

    def to_partner(index, source, landing):
        return pltpu.make_async_remote_copy(
            src_ref=source,
            dst_ref=landing,
            send_sem=xsend_sem.at[index],
            recv_sem=xrecv_sem.at[index],
            device_id=(other_owner, v),
            device_id_type=MESH,
        )

    def integral_place(e, holder):
        at = pl.ds(pl.multiple_of(holder * depth, 16), depth)
        return vvvo_all.at[pl.ds(e * BMAX, BMAX), at, :]

    def integral_copy(e, hop, holder):
        return pltpu.make_async_remote_copy(
            src_ref=vvvo if e == 0 else integral_place(e, v),
            dst_ref=integral_place(e, holder),
            send_sem=vsend_sem.at[e, hop - 1],
            recv_sem=vrecv_sem.at[e, hop - 1],
            device_id=(t, (v + hop) % vir),
            device_id_type=MESH,
        )

    square = split == 2 and ring == 4

    def flipped(number, axis):
        far = 1 << axis
        return number + far * (1 - 2 * ((number // far) % 2))

    def block(e, holder, slot):
        return amps_all.at[((part + e) % split * ring + holder) * BMAX + slot]

    def to_near(e, axis, slot, holder):
        return pltpu.make_async_remote_copy(
            src_ref=amps.at[slot, part_rows(part), :] if e == 0 else block(e, member, slot),
            dst_ref=block(e, holder, slot),
            send_sem=send_sem.at[e, axis, 0, slot],
            recv_sem=recv_sem.at[e, axis, 0, slot],
            device_id=(part * ring + flipped(member, axis), v),
            device_id_type=MESH,
        )

    def way_on(e, slot):
        return 1 if (e, slot) == (0, 0) else 0

    def to_far(e, slot, holder):
        axis = way_on(e, slot)
        return pltpu.make_async_remote_copy(
            src_ref=block(e, holder, slot),
            dst_ref=block(e, holder, slot),
            send_sem=send_sem.at[e, 0, 1, slot],
            recv_sem=recv_sem.at[e, 0, 1, slot],
            device_id=(part * ring + flipped(member, axis), v),
            device_id_type=MESH,
        )

    def pass_on(e, slot):
        axis = 1 - way_on(e, slot)
        to_near(e, axis, slot, flipped(member, axis)).wait_recv()
        to_far(e, slot, flipped(member, axis)).start()

    across = []
    if split == 2:
        across = [
            to_partner(0, triples, triples_all.at[1]),
            to_partner(1, vvvo, integral_place(1, v)),
        ]
    if split == 2:
        for slot in range(BMAX):
            partner_copy(slot, t).start()
    for slot in range(BMAX):
        if square:
            for axis in (1, 0):
                to_near(0, axis, slot, member).start()
        else:
            start_ring(0, 0, slot)
    for copy in across:
        copy.start()
    for hop in range(1, vir):
        integral_copy(0, hop, v).start()
    own = [
        pltpu.make_async_copy(
            amps.at[:, part_rows(part), :], amps_all.at[pl.ds(t * BMAX, BMAX)], own_sem.at[0]
        ),
        pltpu.make_async_copy(vvvo, integral_place(0, v), own_sem.at[1]),
        pltpu.make_async_copy(triples, triples_all.at[0], own_sem.at[2]),
    ]
    for copy in own:
        copy.start()

    if square:
        order = [(6 + 4 * slot, 0, slot) for slot in range(BMAX)]
        order += [(8 * (slot + 1), 1, slot) for slot in range(BMAX)]
        order += [(13 + 8 * slot, 2, slot) for slot in range(BMAX)]
        order += [(25, 3, 0)]
        for _, kind, slot in sorted(order):
            if kind == 0:
                pass_on(0, slot)
            elif kind == 1:
                partner_copy(slot, other_owner).wait_recv()
                for axis in (1, 0):
                    to_near(1, axis, slot, member).start()
            elif kind == 2:
                pass_on(1, slot)
            else:
                for copy in across:
                    copy.wait_recv()
                for hop in range(1, vir):
                    integral_copy(1, hop, v).start()
    elif split == 2:
        for copy in across:
            copy.wait_recv()
        for hop in range(1, vir):
            integral_copy(1, hop, v).start()
        order = [(44 * step + 15 * slot, 0, step, slot) for step in range(1, ring - 1) for slot in range(BMAX)]
        order += [(60 * (slot + 1) + 44 * step, 1, step, slot) for step in range(ring - 1) for slot in range(BMAX)]
        for _, e, step, slot in sorted(order):
            if step == 0:
                partner_copy(slot, other_owner).wait_recv()
                start_ring(1, 0, slot)
            else:
                forward(e, step, slot)
    else:
        def hop_on(step, carry):
            for slot in range(BMAX):
                forward(0, step, slot)
            return carry

        lax.fori_loop(1, ring - 1, hop_on, 0)

    for e in range(split):
        for slot in range(BMAX):
            if square:
                axis = way_on(e, slot)
                to_near(e, axis, slot, flipped(member, axis)).wait_recv()
                to_far(e, slot, ring - 1 - member).wait_recv()
                to_far(e, slot, flipped(member, 1 - axis)).wait_send()
                for axis in range(2):
                    to_near(e, axis, slot, member).wait_send()
                continue
            for way in range(2):
                ring_copy(e, way, ring - 2, slot, arriving=True).wait_recv()
                ring_copy(e, way, 0, slot, first=e == 0).wait_send()

        def drain(step, carry):
            for slot in range(BMAX):
                for way in range(2):
                    ring_copy(e, way, step, slot).wait_send()
            return carry

        if not square:
            lax.fori_loop(1, ring - 1, drain, 0)
        for hop in range(1, vir):
            integral_copy(e, hop, (v + vir - hop) % vir).wait_recv()
            integral_copy(e, hop, v).wait_send()
    if split == 2:
        for copy in across:
            copy.wait_send()
        for slot in range(BMAX):
            partner_copy(slot, t).wait_send()
    for copy in own:
        copy.wait()


def contract_kernel(
    split, tri, sizes_in, roots_in, occ_gap_in, triples_in, pair_gap_in, vir_gap_in, vvvo_in, amps,
    density, grad, sizes, roots, occ_gap, triples, pair_gap, vir_gap, vvvo,
    offsets, rows_in, proj, weights, base, row_sem, load_sem,
):
    loads = [
        pltpu.make_async_copy(source, landing, load_sem.at[index])
        for index, (source, landing) in enumerate(
            [
                (sizes_in, sizes), (roots_in, roots), (occ_gap_in, occ_gap), (triples_in, triples),
                (pair_gap_in, pair_gap), (vir_gap_in, vir_gap), (vvvo_in, vvvo),
            ]
        )
    ]
    for load in loads:
        load.start()
    density[...] = jnp.zeros_like(density)
    weights[...] = jnp.zeros_like(weights)
    for load in loads[:6]:
        load.wait()
    pairs = triples.shape[2]
    occ_count = occ_gap.shape[0]
    rows = amps.shape[1]
    width = vvvo.shape[2]
    layers = split * BMAX
    t = lax.axis_index("tri")
    ring = tri // split

    def fetch(b, start):
        offsets[b] = start

        def one(slot, carry):
            pltpu.make_async_copy(
                amps.at[roots[b] * BMAX + slot], rows_in.at[start + slot], row_sem.at[start + slot]
            ).start()
            return carry

        lax.fori_loop(0, sizes[b], one, 0)
        return start + sizes[b]

    lax.fori_loop(0, tri, fetch, jnp.int32(0))

    def find(owner):
        return lax.fori_loop(
            0, tri, lambda b, found: jnp.where(roots[b] == owner, b, found), jnp.int32(0)
        )

    owned = [find((t + e * ring) % tri) for e in range(split)]
    all_rows = vir_gap.shape[1]
    own_place = lax.broadcasted_iota(jnp.int32, (rows, all_rows), 0) + (t // ring) * rows
    picked = lax.broadcasted_iota(jnp.int32, (rows, all_rows), 1) == own_place
    outer = jnp.sum(jnp.where(picked, vir_gap[...], 0.0), axis=1, keepdims=True) + pair_gap[...]
    for e in range(split):
        for k in range(BMAX):
            own_gap = occ_gap[jnp.minimum(offsets[owned[e]] + k, occ_count - 1)]
            base[e * BMAX + k] = outer + own_gap
    loads[6].wait()
    table = jnp.concatenate([vvvo[layer] for layer in range(layers)], axis=1)
    group = 768 // rows
    span = group * rows

    def stacked(g):
        return rows_in[pl.ds(g * group, group)].reshape(span, rows_in.shape[2])

    def project(g, carry):
        for r in range(group):
            o = g * group + r
            pltpu.make_async_copy(amps.at[0], rows_in.at[o], row_sem.at[o]).wait()
        proj[pl.ds(pl.multiple_of(g * span, span), span), :] = jnp.dot(
            stacked(g), table, preferred_element_type=jnp.float32
        )
        return carry

    lax.fori_loop(0, occ_count // group, project, 0)
    tile = 48
    scale = 1.0 / float(tri * pairs)

    def one_pair(e, q):
        left, right = triples[e, 0, q], triples[e, 1, q]
        left_first, right_first = offsets[left], offsets[right]
        for count in range(1, BMAX + 1):

            @pl.when(sizes[right] == count)
            def _():
                right_gaps = [occ_gap[right_first + j] for j in range(count)]

                def one_k(k, carry):
                    layer = e * BMAX + k
                    lanes = pl.ds(pl.multiple_of(layer * width, width), width)

                    def one_left(i, inner):
                        o = left_first + i
                        left_gap = occ_gap[o]
                        for first in range(0, rows, tile):
                            at = pl.ds(first, tile)
                            here = pl.ds(pl.multiple_of(o * rows, 8) + first, tile)
                            p = proj[here, lanes]
                            den = base[layer, at, :]
                            squares = density[at, :]
                            summed = weights[here, lanes]
                            for j in range(count):
                                there = pl.ds(pl.multiple_of((right_first + j) * rows, 8) + first, tile)
                                d = den + (left_gap + right_gaps[j])
                                r = pl.reciprocal(d, approx=True)
                                r = r * (2.0 - d * r)
                                y = p * proj[there, lanes] * r
                                squares = squares + y * y
                                summed = summed + y
                            density[at, :] = squares
                            weights[here, lanes] = summed
                        return inner

                    return lax.fori_loop(0, sizes[left], one_left, carry)

                lax.fori_loop(0, sizes[owned[e]], one_k, 0)

    for e in range(split):

        def each(q, carry):
            one_pair(e, q)
            return carry

        lax.fori_loop(0, pairs, each, 0)
    density[...] = density[...] * scale

    def product(g):
        left = stacked(g)
        w = weights[pl.ds(g * span, span), :]
        top = w.astype(jnp.bfloat16)
        rest = (w - top.astype(jnp.float32)).astype(jnp.bfloat16)
        over_rows = (((0,), (0,)), ((), ()))
        return lax.dot_general(
            left, top, over_rows, preferred_element_type=jnp.float32
        ) + lax.dot_general(left, rest, over_rows, preferred_element_type=jnp.float32)

    grad[...] = product(0)
    for g in range(1, occ_count // group):
        grad[...] += product(g)


def reduce_kernel(tri, vir, split, grad, dens, grad_out, dens_out, *scratch):
    levels = bits_of(vir)
    came, sums = scratch[:levels], scratch[levels:2 * levels]
    from_partner, dens_in, dens_sum, gsend, grecv, psend, precv, dsend, drecv = scratch[2 * levels:]
    t = lax.axis_index("tri")
    v = lax.axis_index("vir")
    depth, width = grad_out.shape[1:]
    rows = dens.shape[0]
    ring = tri // split
    steps = bits_of(ring)
    other_owner = (t + ring) % tri
    part = t // ring

    def bit(number, level):
        return (number // (1 << level)) % 2

    def flipped(number, level):
        return number + (1 << level) * (1 - 2 * bit(number, level))

    barrier = pltpu.get_barrier_semaphore()
    for level in range(levels):
        pl.semaphore_signal(barrier, inc=1, device_id=(t, flipped(v, level)), device_id_type=MESH)
    for step in range(steps):
        pl.semaphore_signal(barrier, inc=1, device_id=(flipped(t, step), v), device_id_type=MESH)
    if split == 2:
        pl.semaphore_signal(barrier, inc=1, device_id=(other_owner, v), device_id_type=MESH)
    pl.semaphore_wait(barrier, levels + steps + split - 1)

    def lanes(chunk):
        return pl.ds(chunk * width, width)

    def slab(holder):
        return pl.ds(pl.multiple_of(holder * depth, 16), depth)

    def halving(level, chunk, j):
        away = 2 * j + 1 - bit(v, level)
        return pltpu.make_async_remote_copy(
            src_ref=grad.at[slab(away), lanes(chunk)] if level == 0 else sums[level - 1].at[chunk, away],
            dst_ref=came[level].at[chunk, j],
            send_sem=gsend.at[level, chunk, j],
            recv_sem=grecv.at[level, chunk, j],
            device_id=(t, flipped(v, level)),
            device_id_type=MESH,
        )

    def partner_copy(k):
        return pltpu.make_async_remote_copy(
            src_ref=sums[levels - 1].at[BMAX + k, 0],
            dst_ref=from_partner.at[k],
            send_sem=psend.at[k],
            recv_sem=precv.at[k],
            device_id=(other_owner, v),
            device_id_type=MESH,
        )

    def density_copy(step):
        return pltpu.make_async_remote_copy(
            src_ref=dens if step == 0 else dens_sum.at[step - 1],
            dst_ref=dens_in.at[step],
            send_sem=dsend.at[step],
            recv_sem=drecv.at[step],
            device_id=(flipped(t, step), v),
            device_id_type=MESH,
        )

    def part_copy(which):
        at = pl.ds(pl.multiple_of(which * rows, 8), rows)
        return pltpu.make_async_remote_copy(
            src_ref=dens_out.at[at, :],
            dst_ref=dens_out.at[at, :],
            send_sem=dsend.at[steps],
            recv_sem=drecv.at[steps],
            device_id=(other_owner, v),
            device_id_type=MESH,
        )

    chunks = [e * BMAX + k for e in reversed(range(split)) for k in range(BMAX)]
    for chunk in chunks:
        for j in range(vir // 2):
            halving(0, chunk, j).start()
    density_copy(0).start()
    for level in range(levels):
        if level:
            step = level - 1
            if step < steps:
                density_copy(step).wait_recv()
                dens_sum[step] = (dens[...] if step == 0 else dens_sum[step - 1]) + dens_in[step]
                if step + 1 < steps:
                    density_copy(step + 1).start()
        for chunk in chunks:
            for j in range(vir >> (level + 1)):
                halving(level, chunk, j).wait_recv()
                kept = 2 * j + bit(v, level)
                held = grad[slab(kept), lanes(chunk)] if level == 0 else sums[level - 1][chunk, kept]
                sums[level][chunk, j] = held + came[level][chunk, j]
            if level + 1 < levels:
                for j in range(vir >> (level + 2)):
                    halving(level + 1, chunk, j).start()
            elif chunk >= BMAX:
                partner_copy(chunk - BMAX).start()
    for step in range(max(levels - 1, 0), steps):
        density_copy(step).wait_recv()
        dens_sum[step] = (dens[...] if step == 0 else dens_sum[step - 1]) + dens_in[step]
        if step + 1 < steps:
            density_copy(step + 1).start()
    dens_out[pl.ds(pl.multiple_of(part * rows, 8), rows), :] = dens_sum[steps - 1]
    if split == 2:
        part_copy(part).start()
    for k in range(BMAX):
        if split == 2:
            partner_copy(k).wait_recv()
            grad_out[k] = sums[levels - 1][k, 0] + from_partner[k]
        else:
            grad_out[k] = sums[levels - 1][k, 0]
    for level in range(levels):
        for chunk in chunks:
            for j in range(vir >> (level + 1)):
                halving(level, chunk, j).wait_send()
    for step in range(steps):
        density_copy(step).wait_send()
    if split == 2:
        for k in range(BMAX):
            partner_copy(k).wait_send()
        part_copy(1 - part).wait_recv()
        part_copy(part).wait_send()


def body(tri, vir, amps, vvvo, occ_gap, vir_gap, pair_gap, block_sizes, roots, triples):
    own_rows, full = amps.shape[1:]
    depth, width = vvvo.shape[1:]
    pairs = triples.shape[0]
    occ_count = occ_gap.shape[0]
    split = 2 if own_rows % 32 == 0 and tri % 4 == 0 else 1
    ring = tri // split
    rows = own_rows // split
    layers = split * BMAX
    anywhere = pl.BlockSpec(memory_space=pl.ANY)
    in_vmem = pl.BlockSpec(memory_space=pltpu.VMEM)
    in_hbm = pl.BlockSpec(memory_space=pltpu.HBM)
    f32 = jnp.float32
    dma = pltpu.SemaphoreType.DMA
    amps_all, vvvo_all, triples_all = pl.pallas_call(
        functools.partial(gather_kernel, tri, vir, split),
        out_shape=(
            jax.ShapeDtypeStruct((tri * BMAX, rows, full), amps.dtype),
            jax.ShapeDtypeStruct((layers, full, width), vvvo.dtype),
            jax.ShapeDtypeStruct((split, 2, pairs), triples.dtype),
        ),
        in_specs=[anywhere] * 3,
        out_specs=(anywhere,) * 3,
        scratch_shapes=[
            dma((split, 2, ring - 1, BMAX)),
            dma((split, 2, ring - 1, BMAX)),
            dma((BMAX,)),
            dma((BMAX,)),
            dma((split, vir - 1)),
            dma((split, vir - 1)),
            dma((2,)),
            dma((2,)),
            dma((3,)),
        ],
        compiler_params=pltpu.CompilerParams(collective_id=0, has_side_effects=True),
        name="gather_rows",
    )(amps, vvvo, triples.T)
    density, grad = pl.pallas_call(
        functools.partial(contract_kernel, split, tri),
        out_shape=(
            jax.ShapeDtypeStruct((rows, width), f32),
            jax.ShapeDtypeStruct((full, layers * width), f32),
        ),
        in_specs=[in_hbm] * 8,
        out_specs=(in_vmem, in_vmem),
        scratch_shapes=[
            pltpu.SMEM((tri,), jnp.int32),
            pltpu.SMEM((tri,), jnp.int32),
            pltpu.SMEM((occ_count,), f32),
            pltpu.SMEM((split, 2, pairs), jnp.int32),
            pltpu.VMEM((1, width), f32),
            pltpu.VMEM((1, own_rows), f32),
            pltpu.VMEM((layers, full, width), vvvo.dtype),
            pltpu.SMEM((tri,), jnp.int32),
            pltpu.VMEM((occ_count, rows, full), amps.dtype),
            pltpu.VMEM((occ_count * rows, layers * width), f32),
            pltpu.VMEM((occ_count * rows, layers * width), f32),
            pltpu.VMEM((layers, rows, width), f32),
            dma((occ_count,)),
            dma((7,)),
        ],
        compiler_params=pltpu.CompilerParams(vmem_limit_bytes=48 << 20),
        name="contract_pairs",
    )(block_sizes, roots, occ_gap, triples_all, pair_gap[None, :], vir_gap[None, :], vvvo_all, amps_all)
    steps = bits_of(ring)
    levels = bits_of(vir)
    halves = [(layers, vir >> (level + 1), depth, width) for level in range(levels)]
    grad_share, density_all = pl.pallas_call(
        functools.partial(reduce_kernel, tri, vir, split),
        out_shape=(
            jax.ShapeDtypeStruct((BMAX, depth, width), f32),
            jax.ShapeDtypeStruct((own_rows, width), f32),
        ),
        in_specs=[in_vmem] * 2,
        out_specs=(in_vmem, in_vmem),
        scratch_shapes=[pltpu.VMEM(shape, f32) for shape in halves + halves]
        + [
            pltpu.VMEM((BMAX, depth, width), f32),
            pltpu.VMEM((steps, rows, width), f32),
            pltpu.VMEM((steps, rows, width), f32),
            dma((levels, layers, vir // 2)),
            dma((levels, layers, vir // 2)),
            dma((BMAX,)),
            dma((BMAX,)),
            dma((steps + 1,)),
            dma((steps + 1,)),
        ],
        compiler_params=pltpu.CompilerParams(
            collective_id=1, has_side_effects=True, vmem_limit_bytes=24 << 20
        ),
        name="reduce_sums",
    )(grad, density)
    return density_all, grad_share


def solution(mesh):
    return jax.shard_map(
        functools.partial(body, mesh.shape["tri"], mesh.shape["vir"]),
        mesh=mesh,
        in_specs=(
            P("tri", "vir", None),
            P("tri", "vir", None),
            P(),
            P("vir"),
            P(),
            P(),
            P(),
            P("tri", None),
        ),
        out_specs=(P("vir", None), P("tri", "vir", None)),
        check_vma=False,
    )
```

```python
import functools

import jax
import jax.numpy as jnp
from jax import lax
from jax.experimental import pallas as pl
from jax.experimental.pallas import tpu as pltpu
from jax.sharding import PartitionSpec as P

BMAX = 3
MESH = pl.DeviceIdType.MESH


def bits_of(count):
    return count.bit_length() - 1


def gather_kernel(
    tri, vir, split, amps, vvvo, triples, amps_all, vvvo_all, triples_all,
    send_sem, recv_sem, psend_sem, precv_sem, vsend_sem, vrecv_sem, xsend_sem, xrecv_sem, own_sem,
):
    t = lax.axis_index("tri")
    v = lax.axis_index("vir")
    ring = tri // split
    part = t // ring
    member = t % ring
    other_owner = (t + ring) % tri
    depth = vvvo.shape[1]
    rows = amps.shape[1] // split
    columns = amps.shape[2] // 2
    odd = member % 2
    place = odd * (ring - 1 - member // 2) + (1 - odd) * (member // 2)

    def member_at(where):
        where = where % ring
        back = where // (ring // 2)
        return (1 - back) * 2 * where + back * (2 * (ring - 1 - where) + 1)

    toward = tuple(part * ring + member_at(place + step) for step in (1, ring - 1))

    barrier = pltpu.get_barrier_semaphore()
    for other in toward:
        pl.semaphore_signal(barrier, inc=1, device_id=(other, v), device_id_type=MESH)
    for hop in range(1, vir):
        pl.semaphore_signal(barrier, inc=1, device_id=(t, (v + hop) % vir), device_id_type=MESH)
    if split == 2:
        pl.semaphore_signal(barrier, inc=1, device_id=(other_owner, v), device_id_type=MESH)
    pl.semaphore_wait(barrier, 2 + vir - 1 + split - 1)

    def part_rows(which):
        return pl.ds(pl.multiple_of(which * rows, 16), rows)

    def ring_copy(e, way, step, slot, arriving=False, first=False):
        shift = step + 1 if arriving else step
        source = member_at(place + ring - shift) if way == 0 else member_at(place + shift)
        half = (part + e) % split
        cols = pl.ds(way * columns, columns)
        landing = amps_all.at[(half * ring + source) * BMAX + slot, :, cols]
        return pltpu.make_async_remote_copy(
            src_ref=amps.at[slot, part_rows(part), cols] if first else landing,
            dst_ref=landing,
            send_sem=send_sem.at[e, way, step, slot],
            recv_sem=recv_sem.at[e, way, step, slot],
            device_id=(toward[way], v),
            device_id_type=MESH,
        )

    def start_ring(e, step, slot):
        for way in range(2):
            ring_copy(e, way, step, slot, first=e == 0).start()

    def forward(e, step, slot):
        for way in range(2):
            ring_copy(e, way, step - 1, slot, arriving=True).wait_recv()
            ring_copy(e, way, step, slot).start()

    def partner_copy(slot, owner):
        return pltpu.make_async_remote_copy(
            src_ref=amps.at[slot, part_rows((part + 1) % split), :],
            dst_ref=amps_all.at[owner * BMAX + slot],
            send_sem=psend_sem.at[slot],
            recv_sem=precv_sem.at[slot],
            device_id=(other_owner, v),
            device_id_type=MESH,
        )

    def to_partner(index, source, landing):
        return pltpu.make_async_remote_copy(
            src_ref=source,
            dst_ref=landing,
            send_sem=xsend_sem.at[index],
            recv_sem=xrecv_sem.at[index],
            device_id=(other_owner, v),
            device_id_type=MESH,
        )

    def integral_place(e, holder):
        at = pl.ds(pl.multiple_of(holder * depth, 16), depth)
        return vvvo_all.at[pl.ds(e * BMAX, BMAX), at, :]

    def integral_copy(e, hop, holder):
        return pltpu.make_async_remote_copy(
            src_ref=vvvo if e == 0 else integral_place(e, v),
            dst_ref=integral_place(e, holder),
            send_sem=vsend_sem.at[e, hop - 1],
            recv_sem=vrecv_sem.at[e, hop - 1],
            device_id=(t, (v + hop) % vir),
            device_id_type=MESH,
        )

    square = split == 2 and ring == 4

    def flipped(number, axis):
        far = 1 << axis
        return number + far * (1 - 2 * ((number // far) % 2))

    def block(e, holder, slot):
        return amps_all.at[((part + e) % split * ring + holder) * BMAX + slot]

    def to_near(e, axis, slot, holder):
        return pltpu.make_async_remote_copy(
            src_ref=amps.at[slot, part_rows(part), :] if e == 0 else block(e, member, slot),
            dst_ref=block(e, holder, slot),
            send_sem=send_sem.at[e, axis, 0, slot],
            recv_sem=recv_sem.at[e, axis, 0, slot],
            device_id=(part * ring + flipped(member, axis), v),
            device_id_type=MESH,
        )

    def way_on(e, slot):
        return 1 if (e, slot) == (0, 0) else 0

    def to_far(e, slot, holder):
        axis = way_on(e, slot)
        return pltpu.make_async_remote_copy(
            src_ref=block(e, holder, slot),
            dst_ref=block(e, holder, slot),
            send_sem=send_sem.at[e, 0, 1, slot],
            recv_sem=recv_sem.at[e, 0, 1, slot],
            device_id=(part * ring + flipped(member, axis), v),
            device_id_type=MESH,
        )

    def pass_on(e, slot):
        axis = 1 - way_on(e, slot)
        to_near(e, axis, slot, flipped(member, axis)).wait_recv()
        to_far(e, slot, flipped(member, axis)).start()

    across = []
    if split == 2:
        across = [
            to_partner(0, triples, triples_all.at[1]),
            to_partner(1, vvvo, integral_place(1, v)),
        ]
    if square:
        partner_copy(0, t).start()
        to_near(0, 1, 0, member).start()
        for slot in range(BMAX):
            to_near(0, 0, slot, member).start()
    else:
        for slot in range(BMAX):
            if split == 2:
                partner_copy(slot, t).start()
            start_ring(0, 0, slot)
        for copy in across:
            copy.start()
    for hop in range(1, vir):
        integral_copy(0, hop, v).start()
    own = [
        pltpu.make_async_copy(
            amps.at[:, part_rows(part), :], amps_all.at[pl.ds(t * BMAX, BMAX)], own_sem.at[0]
        ),
        pltpu.make_async_copy(vvvo, integral_place(0, v), own_sem.at[1]),
        pltpu.make_async_copy(triples, triples_all.at[0], own_sem.at[2]),
    ]
    for copy in own:
        copy.start()

    if square:
        order = [(6, 0, 0), (12, 0, 1), (19, 0, 2)]
        order += [(8 + 7 * slot, 1, slot) for slot in range(BMAX)]
        order += [(14, 2, 0), (22, 2, 1), (28, 2, 2), (30, 4, 0)]
        order += [(7, 3, 0), (13, 3, 1), (20, 3, 2)]
        for _, kind, slot in sorted(order):
            if kind == 0:
                pass_on(0, slot)
            elif kind == 1:
                partner_copy(slot, other_owner).wait_recv()
                for axis in (1, 0):
                    to_near(1, axis, slot, member).start()
            elif kind == 2:
                pass_on(1, slot)
            elif kind == 3:
                partner_copy(slot, t).wait_send()
                if slot + 1 < BMAX:
                    partner_copy(slot + 1, t).start()
                    to_near(0, 1, slot + 1, member).start()
                else:
                    for copy in across:
                        copy.start()
            else:
                for copy in across:
                    copy.wait_recv()
                for hop in range(1, vir):
                    integral_copy(1, hop, v).start()
    elif split == 2:
        for copy in across:
            copy.wait_recv()
        for hop in range(1, vir):
            integral_copy(1, hop, v).start()
        order = [(44 * step + 15 * slot, 0, step, slot) for step in range(1, ring - 1) for slot in range(BMAX)]
        order += [(60 * (slot + 1) + 44 * step, 1, step, slot) for step in range(ring - 1) for slot in range(BMAX)]
        for _, e, step, slot in sorted(order):
            if step == 0:
                partner_copy(slot, other_owner).wait_recv()
                start_ring(1, 0, slot)
            else:
                forward(e, step, slot)
    else:
        def hop_on(step, carry):
            for slot in range(BMAX):
                forward(0, step, slot)
            return carry

        lax.fori_loop(1, ring - 1, hop_on, 0)

    for e in range(split):
        for slot in range(BMAX):
            if square:
                axis = way_on(e, slot)
                to_near(e, axis, slot, flipped(member, axis)).wait_recv()
                to_far(e, slot, ring - 1 - member).wait_recv()
                to_far(e, slot, flipped(member, 1 - axis)).wait_send()
                for axis in range(2):
                    to_near(e, axis, slot, member).wait_send()
                continue
            for way in range(2):
                ring_copy(e, way, ring - 2, slot, arriving=True).wait_recv()
                ring_copy(e, way, 0, slot, first=e == 0).wait_send()

        def drain(step, carry):
            for slot in range(BMAX):
                for way in range(2):
                    ring_copy(e, way, step, slot).wait_send()
            return carry

        if not square:
            lax.fori_loop(1, ring - 1, drain, 0)
        for hop in range(1, vir):
            integral_copy(e, hop, (v + vir - hop) % vir).wait_recv()
            integral_copy(e, hop, v).wait_send()
    if split == 2:
        for copy in across:
            copy.wait_send()
        if not square:
            for slot in range(BMAX):
                partner_copy(slot, t).wait_send()
    for copy in own:
        copy.wait()


def contract_kernel(
    split, tri, sizes_in, roots_in, occ_gap_in, triples_in, pair_gap_in, vir_gap_in, vvvo_in, amps,
    density, grad, sizes, roots, occ_gap, triples, pair_gap, vir_gap, vvvo,
    offsets, rows_in, proj, weights, base, row_sem, load_sem,
):
    loads = [
        pltpu.make_async_copy(source, landing, load_sem.at[index])
        for index, (source, landing) in enumerate(
            [
                (sizes_in, sizes), (roots_in, roots), (occ_gap_in, occ_gap), (triples_in, triples),
                (pair_gap_in, pair_gap), (vir_gap_in, vir_gap), (vvvo_in, vvvo),
            ]
        )
    ]
    for load in loads:
        load.start()
    density[...] = jnp.zeros_like(density)
    weights[...] = jnp.zeros_like(weights)
    for load in loads[:6]:
        load.wait()
    pairs = triples.shape[2]
    occ_count = occ_gap.shape[0]
    rows = amps.shape[1]
    width = vvvo.shape[2]
    layers = split * BMAX
    t = lax.axis_index("tri")
    ring = tri // split

    def fetch(b, start):
        offsets[b] = start

        def one(slot, carry):
            pltpu.make_async_copy(
                amps.at[roots[b] * BMAX + slot], rows_in.at[start + slot], row_sem.at[start + slot]
            ).start()
            return carry

        lax.fori_loop(0, sizes[b], one, 0)
        return start + sizes[b]

    lax.fori_loop(0, tri, fetch, jnp.int32(0))

    def find(owner):
        return lax.fori_loop(
            0, tri, lambda b, found: jnp.where(roots[b] == owner, b, found), jnp.int32(0)
        )

    owned = [find((t + e * ring) % tri) for e in range(split)]
    all_rows = vir_gap.shape[1]
    own_place = lax.broadcasted_iota(jnp.int32, (rows, all_rows), 0) + (t // ring) * rows
    picked = lax.broadcasted_iota(jnp.int32, (rows, all_rows), 1) == own_place
    outer = jnp.sum(jnp.where(picked, vir_gap[...], 0.0), axis=1, keepdims=True) + pair_gap[...]
    for e in range(split):
        for k in range(BMAX):
            own_gap = occ_gap[jnp.minimum(offsets[owned[e]] + k, occ_count - 1)]
            base[e * BMAX + k] = outer + own_gap
    loads[6].wait()
    table = jnp.concatenate([vvvo[layer] for layer in range(layers)], axis=1)
    group = 768 // rows
    span = group * rows

    def stacked(g):
        return rows_in[pl.ds(g * group, group)].reshape(span, rows_in.shape[2])

    def project(g, carry):
        for r in range(group):
            o = g * group + r
            pltpu.make_async_copy(amps.at[0], rows_in.at[o], row_sem.at[o]).wait()
        proj[pl.ds(pl.multiple_of(g * span, span), span), :] = jnp.dot(
            stacked(g), table, preferred_element_type=jnp.float32
        )
        return carry

    lax.fori_loop(0, occ_count // group, project, 0)
    tile = 48
    scale = 1.0 / float(tri * pairs)

    def one_pair(e, q):
        left, right = triples[e, 0, q], triples[e, 1, q]
        left_first, right_first = offsets[left], offsets[right]
        for count in range(1, BMAX + 1):

            @pl.when(sizes[right] == count)
            def _():
                right_gaps = [occ_gap[right_first + j] for j in range(count)]

                def one_k(k, carry):
                    layer = e * BMAX + k
                    lanes = pl.ds(pl.multiple_of(layer * width, width), width)

                    def one_left(i, inner):
                        o = left_first + i
                        left_gap = occ_gap[o]
                        for first in range(0, rows, tile):
                            at = pl.ds(first, tile)
                            here = pl.ds(pl.multiple_of(o * rows, 8) + first, tile)
                            p = proj[here, lanes]
                            den = base[layer, at, :]
                            squares = density[at, :]
                            summed = weights[here, lanes]
                            for j in range(count):
                                there = pl.ds(pl.multiple_of((right_first + j) * rows, 8) + first, tile)
                                d = den + (left_gap + right_gaps[j])
                                r = pl.reciprocal(d, approx=True)
                                r = r * (2.0 - d * r)
                                y = p * proj[there, lanes] * r
                                squares = squares + y * y
                                summed = summed + y
                            density[at, :] = squares
                            weights[here, lanes] = summed
                        return inner

                    return lax.fori_loop(0, sizes[left], one_left, carry)

                lax.fori_loop(0, sizes[owned[e]], one_k, 0)

    for e in range(split):

        def each(q, carry):
            one_pair(e, q)
            return carry

        lax.fori_loop(0, pairs, each, 0)
    density[...] = density[...] * scale

    def product(g):
        left = stacked(g)
        w = weights[pl.ds(g * span, span), :]
        top = w.astype(jnp.bfloat16)
        rest = (w - top.astype(jnp.float32)).astype(jnp.bfloat16)
        over_rows = (((0,), (0,)), ((), ()))
        return lax.dot_general(
            left, top, over_rows, preferred_element_type=jnp.float32
        ) + lax.dot_general(left, rest, over_rows, preferred_element_type=jnp.float32)

    grad[...] = product(0)
    for g in range(1, occ_count // group):
        grad[...] += product(g)


def reduce_kernel(tri, vir, split, grad, dens, grad_out, dens_out, *scratch):
    levels = bits_of(vir)
    came, sums = scratch[:levels], scratch[levels:2 * levels]
    from_partner, dens_in, dens_sum, gsend, grecv, psend, precv, dsend, drecv = scratch[2 * levels:]
    t = lax.axis_index("tri")
    v = lax.axis_index("vir")
    depth, width = grad_out.shape[1:]
    rows = dens.shape[0]
    ring = tri // split
    steps = bits_of(ring)
    other_owner = (t + ring) % tri
    part = t // ring

    def bit(number, level):
        return (number // (1 << level)) % 2

    def flipped(number, level):
        return number + (1 << level) * (1 - 2 * bit(number, level))

    barrier = pltpu.get_barrier_semaphore()
    for level in range(levels):
        pl.semaphore_signal(barrier, inc=1, device_id=(t, flipped(v, level)), device_id_type=MESH)
    for step in range(steps):
        pl.semaphore_signal(barrier, inc=1, device_id=(flipped(t, step), v), device_id_type=MESH)
    if split == 2:
        pl.semaphore_signal(barrier, inc=1, device_id=(other_owner, v), device_id_type=MESH)
    pl.semaphore_wait(barrier, levels + steps + split - 1)

    def lanes(chunk):
        return pl.ds(chunk * width, width)

    def slab(holder):
        return pl.ds(pl.multiple_of(holder * depth, 16), depth)

    def halving(level, chunk, j):
        away = 2 * j + 1 - bit(v, level)
        return pltpu.make_async_remote_copy(
            src_ref=grad.at[slab(away), lanes(chunk)] if level == 0 else sums[level - 1].at[chunk, away],
            dst_ref=came[level].at[chunk, j],
            send_sem=gsend.at[level, chunk, j],
            recv_sem=grecv.at[level, chunk, j],
            device_id=(t, flipped(v, level)),
            device_id_type=MESH,
        )

    def partner_copy(k):
        return pltpu.make_async_remote_copy(
            src_ref=sums[levels - 1].at[BMAX + k, 0],
            dst_ref=from_partner.at[k],
            send_sem=psend.at[k],
            recv_sem=precv.at[k],
            device_id=(other_owner, v),
            device_id_type=MESH,
        )

    def density_copy(step):
        return pltpu.make_async_remote_copy(
            src_ref=dens if step == 0 else dens_sum.at[step - 1],
            dst_ref=dens_in.at[step],
            send_sem=dsend.at[step],
            recv_sem=drecv.at[step],
            device_id=(flipped(t, step), v),
            device_id_type=MESH,
        )

    def part_copy(which):
        at = pl.ds(pl.multiple_of(which * rows, 8), rows)
        return pltpu.make_async_remote_copy(
            src_ref=dens_out.at[at, :],
            dst_ref=dens_out.at[at, :],
            send_sem=dsend.at[steps],
            recv_sem=drecv.at[steps],
            device_id=(other_owner, v),
            device_id_type=MESH,
        )

    chunks = [e * BMAX + k for e in reversed(range(split)) for k in range(BMAX)]
    for chunk in chunks:
        for j in range(vir // 2):
            halving(0, chunk, j).start()
    density_copy(0).start()
    def add_density(step):
        density_copy(step).wait_recv()
        dens_sum[step] = (dens[...] if step == 0 else dens_sum[step - 1]) + dens_in[step]
        if step + 1 < steps:
            density_copy(step + 1).start()

    ahead = 2
    for level in range(levels):
        last = level + 1 == levels
        for index, chunk in enumerate(chunks):
            for j in range(vir >> (level + 1)):
                halving(level, chunk, j).wait_recv()
                if level and last and index + ahead < len(chunks):
                    halving(level, chunks[index + ahead], j).start()
                kept = 2 * j + bit(v, level)
                held = grad[slab(kept), lanes(chunk)] if level == 0 else sums[level - 1][chunk, kept]
                sums[level][chunk, j] = held + came[level][chunk, j]
            if not last:
                if level + 2 < levels or index < ahead:
                    for j in range(vir >> (level + 2)):
                        halving(level + 1, chunk, j).start()
            elif chunk >= BMAX:
                partner_copy(chunk - BMAX).start()
            if level and index == BMAX - 1 and level - 1 < steps:
                add_density(level - 1)
    for step in range(max(levels - 1, 0), steps):
        add_density(step)
    dens_out[pl.ds(pl.multiple_of(part * rows, 8), rows), :] = dens_sum[steps - 1]
    if split == 2:
        part_copy(part).start()
    for k in range(BMAX):
        if split == 2:
            partner_copy(k).wait_recv()
            grad_out[k] = sums[levels - 1][k, 0] + from_partner[k]
        else:
            grad_out[k] = sums[levels - 1][k, 0]
    for level in range(levels):
        for chunk in chunks:
            for j in range(vir >> (level + 1)):
                halving(level, chunk, j).wait_send()
    for step in range(steps):
        density_copy(step).wait_send()
    if split == 2:
        for k in range(BMAX):
            partner_copy(k).wait_send()
        part_copy(1 - part).wait_recv()
        part_copy(part).wait_send()


def body(tri, vir, amps, vvvo, occ_gap, vir_gap, pair_gap, block_sizes, roots, triples):
    own_rows, full = amps.shape[1:]
    depth, width = vvvo.shape[1:]
    pairs = triples.shape[0]
    occ_count = occ_gap.shape[0]
    split = 2 if own_rows % 32 == 0 and tri % 4 == 0 else 1
    ring = tri // split
    rows = own_rows // split
    layers = split * BMAX
    anywhere = pl.BlockSpec(memory_space=pl.ANY)
    in_vmem = pl.BlockSpec(memory_space=pltpu.VMEM)
    in_hbm = pl.BlockSpec(memory_space=pltpu.HBM)
    f32 = jnp.float32
    dma = pltpu.SemaphoreType.DMA
    amps_all, vvvo_all, triples_all = pl.pallas_call(
        functools.partial(gather_kernel, tri, vir, split),
        out_shape=(
            jax.ShapeDtypeStruct((tri * BMAX, rows, full), amps.dtype),
            jax.ShapeDtypeStruct((layers, full, width), vvvo.dtype),
            jax.ShapeDtypeStruct((split, 2, pairs), triples.dtype),
        ),
        in_specs=[anywhere] * 3,
        out_specs=(anywhere,) * 3,
        scratch_shapes=[
            dma((split, 2, ring - 1, BMAX)),
            dma((split, 2, ring - 1, BMAX)),
            dma((BMAX,)),
            dma((BMAX,)),
            dma((split, vir - 1)),
            dma((split, vir - 1)),
            dma((2,)),
            dma((2,)),
            dma((3,)),
        ],
        compiler_params=pltpu.CompilerParams(collective_id=0, has_side_effects=True),
        name="gather_rows",
    )(amps, vvvo, triples.T)
    density, grad = pl.pallas_call(
        functools.partial(contract_kernel, split, tri),
        out_shape=(
            jax.ShapeDtypeStruct((rows, width), f32),
            jax.ShapeDtypeStruct((full, layers * width), f32),
        ),
        in_specs=[in_hbm] * 8,
        out_specs=(in_vmem, in_vmem),
        scratch_shapes=[
            pltpu.SMEM((tri,), jnp.int32),
            pltpu.SMEM((tri,), jnp.int32),
            pltpu.SMEM((occ_count,), f32),
            pltpu.SMEM((split, 2, pairs), jnp.int32),
            pltpu.VMEM((1, width), f32),
            pltpu.VMEM((1, own_rows), f32),
            pltpu.VMEM((layers, full, width), vvvo.dtype),
            pltpu.SMEM((tri,), jnp.int32),
            pltpu.VMEM((occ_count, rows, full), amps.dtype),
            pltpu.VMEM((occ_count * rows, layers * width), f32),
            pltpu.VMEM((occ_count * rows, layers * width), f32),
            pltpu.VMEM((layers, rows, width), f32),
            dma((occ_count,)),
            dma((7,)),
        ],
        compiler_params=pltpu.CompilerParams(vmem_limit_bytes=60 << 20),
        name="contract_pairs",
    )(block_sizes, roots, occ_gap, triples_all, pair_gap[None, :], vir_gap[None, :], vvvo_all, amps_all)
    steps = bits_of(ring)
    levels = bits_of(vir)
    halves = [(layers, vir >> (level + 1), depth, width) for level in range(levels)]
    grad_share, density_all = pl.pallas_call(
        functools.partial(reduce_kernel, tri, vir, split),
        out_shape=(
            jax.ShapeDtypeStruct((BMAX, depth, width), f32),
            jax.ShapeDtypeStruct((own_rows, width), f32),
        ),
        in_specs=[in_vmem] * 2,
        out_specs=(in_vmem, in_vmem),
        scratch_shapes=[pltpu.VMEM(shape, f32) for shape in halves + halves]
        + [
            pltpu.VMEM((BMAX, depth, width), f32),
            pltpu.VMEM((steps, rows, width), f32),
            pltpu.VMEM((steps, rows, width), f32),
            dma((levels, layers, vir // 2)),
            dma((levels, layers, vir // 2)),
            dma((BMAX,)),
            dma((BMAX,)),
            dma((steps + 1,)),
            dma((steps + 1,)),
        ],
        compiler_params=pltpu.CompilerParams(
            collective_id=1, has_side_effects=True, vmem_limit_bytes=24 << 20
        ),
        name="reduce_sums",
    )(grad, density)
    return density_all, grad_share


def solution(mesh):
    return jax.shard_map(
        functools.partial(body, mesh.shape["tri"], mesh.shape["vir"]),
        mesh=mesh,
        in_specs=(
            P("tri", "vir", None),
            P("tri", "vir", None),
            P(),
            P("vir"),
            P(),
            P(),
            P(),
            P("tri", None),
        ),
        out_specs=(P("vir", None), P("tri", "vir", None)),
        check_vma=False,
    )
```
